128 devices in a mesh: seq: 64 (over y, z_hi, x, core), head: 2 (over z_lo).
Axes of the slice: x: 4, y: 4, z: 4 (z_hi: 2, z_lo: 2; z = z_hi * 2 + z_lo), core: 2. Of those that a mesh axis runs over, the one named last changes fastest.
Arguments:
- queries: bfloat16 [16384, 4096], P('seq', 'head'), may hold values from -8 to 8
- keys: bfloat16 [16384, 1024], P('seq', 'head'), may hold values from -8 to 8
- values: bfloat16 [16384, 1024], P('seq', 'head'), may hold values from -8 to 8
- gate_logit: float32 [32], P('head'), may hold values from -3 to 3
- out_weight: bfloat16 [4096, 4096], P('head'), may hold values from -0.09375 to 0.09375
Outputs:
- layer_out: bfloat16 [16384, 4096], P('seq', 'head')
The draws below stay inside these ranges and needn't reach their ends.
All inputs are finite; a program needn't handle non-finite values.
Results may differ from the reference program's by a relative error of at most 0.0095.
Values may be sent and summed in bfloat16 or wider, within the bound.
No kernel may reach another device: no remote copies, remote signals or barrier semaphores. Data moves between devices by JAX's collectives and lax.ppermute only.
A program may use at most 256 MiB of HBM per device.

```python
import math
import jax
import jax.numpy as jnp
from jax import lax

D = 4096
Q_HEADS = 32
KV_HEADS = 8
HDIM = 128
WINDOW = 4096
SEG = 1024
TOK_DEV = 256
TOKENS = 16384


def draw_queries(key, part):
    base_key = jax.random.fold_in(key, 11)
    base_draw = jnp.clip(0.6 * jax.random.normal(base_key, (TOKENS, Q_HEADS, HDIM), jnp.float32), -8.0, 8.0)
    return base_draw.reshape(TOKENS, Q_HEADS * HDIM).astype(jnp.bfloat16)


def draw_keys(key, part):
    scale_key = jax.random.fold_in(key, 21)
    token_key = jax.random.fold_in(key, 22)
    base_key = jax.random.fold_in(key, 23)
    block_scale = jnp.exp(jax.random.uniform(scale_key, (TOKENS // TOK_DEV, KV_HEADS), jnp.float32, math.log(0.3), math.log(3.0)))
    block_scale = jnp.repeat(block_scale, TOK_DEV, axis=0)
    token_scale = jnp.exp(jax.random.uniform(token_key, (TOKENS, KV_HEADS), jnp.float32, math.log(0.6), math.log(1.6)))
    row_scale = (block_scale * token_scale)[:, :, None]
    base_draw = jax.random.normal(base_key, (TOKENS, KV_HEADS, HDIM), jnp.float32)
    base_draw = jnp.clip(base_draw * row_scale, -8.0, 8.0)
    return base_draw.reshape(TOKENS, KV_HEADS * HDIM).astype(jnp.bfloat16)


def draw_values(key, part):
    offset_key = jax.random.fold_in(key, 31)
    base_key = jax.random.fold_in(key, 32)
    offsets = jax.random.uniform(offset_key, (TOKENS // TOK_DEV, KV_HEADS * HDIM), jnp.float32, -1.0, 1.0)
    offsets = jnp.repeat(offsets, TOK_DEV, axis=0)
    base_draw = jax.random.normal(base_key, (TOKENS, KV_HEADS * HDIM), jnp.float32)
    return jnp.clip(base_draw + offsets, -8.0, 8.0).astype(jnp.bfloat16)


def steps_of(rng, shape, split, smallest, largest):
    gain = 1.0
    for position, blocks in split:
        draws = jax.random.uniform(jax.random.fold_in(jax.random.fold_in(rng, 6), position), (blocks,), jnp.float32, smallest / len(split), largest / len(split))
        gain = gain * jnp.repeat(jnp.exp(draws), shape[position] // blocks).reshape((-1,) + (1,) * (len(shape) - 1 - position))
    return gain


def gaussian(key, extent, scale, bound, cuts=(), held_as=jnp.bfloat16):
    drawn = scale * jax.random.normal(key, extent, jnp.float32)
    if cuts:
        drawn = drawn * steps_of(key, extent, cuts, -0.22, 0.18)
    return jnp.clip(drawn, -bound, bound).astype(held_as)


def setup_inputs(seed: int = 0) -> dict:
    seeds = jax.random.split(jax.random.key(seed), 6)
    return {
        "queries": draw_queries(jax.random.fold_in(seeds[5], 71), 0),
        "keys": draw_keys(jax.random.fold_in(seeds[5], 71), 0),
        "values": draw_values(jax.random.fold_in(seeds[5], 71), 0),
        "gate_logit": jnp.clip(jax.random.uniform(seeds[3], (Q_HEADS,), jnp.float32, -3.0, 3.0) * steps_of(seeds[3], (Q_HEADS,), ((0, 2),), -0.4, 0.0), -3.0, 3.0),
        "out_weight": gaussian(seeds[4], (Q_HEADS * HDIM, D), (Q_HEADS * HDIM) ** -0.5, 0.09375, ((0, 2),)),
    }


def feature(source):
    return jax.nn.elu(source.astype(jnp.float32)) + 1.0

def reference(queries, keys, values, gate_logit, out_weight):
    group_size = Q_HEADS // KV_HEADS
    score_scale = 1.0 / math.sqrt(HDIM)
    query_four = queries.reshape(TOKENS, KV_HEADS, group_size, HDIM)
    key_three = keys.reshape(TOKENS, KV_HEADS, HDIM)
    value_three = values.reshape(TOKENS, KV_HEADS, HDIM)
    padding = jnp.zeros((WINDOW, KV_HEADS, HDIM), jnp.bfloat16)
    key_padded = jnp.concatenate([padding, key_three], 0)
    value_padded = jnp.concatenate([padding, value_three], 0)

    def attend_block(block):
        first = (block * TOK_DEV).astype(jnp.int32)
        query_rows = lax.dynamic_slice_in_dim(query_four, first, TOK_DEV, 0).astype(jnp.float32)
        key_rows = lax.dynamic_slice_in_dim(key_padded, first, WINDOW + TOK_DEV, 0).astype(jnp.float32)
        value_rows = lax.dynamic_slice_in_dim(value_padded, first, WINDOW + TOK_DEV, 0).astype(jnp.float32)
        query_pos = first + jnp.arange(TOK_DEV, dtype=jnp.int32)
        key_pos = first - WINDOW + jnp.arange(WINDOW + TOK_DEV, dtype=jnp.int32)
        distance = query_pos[:, None] - key_pos[None, :]
        allowed = (distance >= 0) & (distance < WINDOW) & (key_pos[None, :] >= 0)
        scores = jnp.einsum('tgrd,sgd->tgrs', query_rows, key_rows) * score_scale
        scores = jnp.where(allowed[:, None, None, :], scores, jnp.float32(-1e+30))
        peak = lax.optimization_barrier(jnp.max(scores, axis=-1, keepdims=True))
        weights = jnp.exp(scores - peak)
        sum_total = lax.optimization_barrier(jnp.sum(weights, axis=-1))
        low = weights.astype(jnp.bfloat16).astype(jnp.float32)
        weighted = jnp.einsum('tgrs,sgd->tgrd', low, value_rows)
        return weighted / sum_total[..., None]
    local_out = lax.map(attend_block, jnp.arange(TOKENS // TOK_DEV, dtype=jnp.int32))
    local_out = local_out.reshape(TOKENS, KV_HEADS, group_size, HDIM)
    seg_count = TOKENS // SEG
    key_feature = feature(key_three).astype(jnp.bfloat16).astype(jnp.float32).reshape(seg_count, SEG, KV_HEADS, HDIM)
    value_seg = value_three.astype(jnp.float32).reshape(seg_count, SEG, KV_HEADS, HDIM)
    delta_memory = jnp.einsum('nsgd,nsge->ngde', key_feature, value_seg, precision=lax.Precision.HIGHEST)
    delta_norm = lax.optimization_barrier(jnp.sum(key_feature, axis=1))
    memory = jnp.concatenate([jnp.zeros((1, KV_HEADS, HDIM, HDIM), jnp.float32), jnp.cumsum(delta_memory, 0)[:-1]], 0)
    key_total = jnp.concatenate([jnp.zeros((1, KV_HEADS, HDIM), jnp.float32), jnp.cumsum(delta_norm, 0)[:-1]], 0)
    query_feature = feature(query_four).astype(jnp.bfloat16).astype(jnp.float32).reshape(seg_count, SEG, KV_HEADS, group_size, HDIM)
    recalled = jnp.einsum('nsgrd,ngde->nsgre', query_feature, memory, precision=lax.Precision.HIGHEST)
    denominator = 1.0 + jnp.einsum('nsgrd,ngd->nsgr', query_feature, key_total, precision=lax.Precision.HIGHEST)
    retrieved = (recalled / denominator[..., None]).reshape(TOKENS, KV_HEADS, group_size, HDIM)
    gate_share = jax.nn.sigmoid(gate_logit.astype(jnp.float32)).reshape(KV_HEADS, group_size)[None, :, :, None]
    mixed = (gate_share * retrieved + (1.0 - gate_share) * local_out).astype(jnp.bfloat16)
    mixed = mixed.reshape(TOKENS, Q_HEADS * HDIM)
    return jnp.dot(mixed, out_weight, preferred_element_type=jnp.float32).astype(jnp.bfloat16)
```

```python
import functools
import math

import jax
import jax.numpy as jnp
from jax import lax
from jax.experimental import pallas as pl
from jax.experimental.pallas import tpu as pltpu
from jax.sharding import PartitionSpec as P

HDIM = 128
WINDOW = 4096
SEG = 1024
BLK = 256
GROUP = 4
BACK = WINDOW // SEG
SPAN = WINDOW + SEG
SCALE = math.log2(math.e) / math.sqrt(HDIM)
CHUNKS = ((0, 128), (128, 64), (192, 64))
TIE_MEM = False
KEYS_STEP = 512
BF = jnp.bfloat16
F32 = jnp.float32
LAST = (((1,), (1,)), ((), ()))
MB = 1 << 20


def whole(shape):
    return pl.BlockSpec(shape, lambda *_: (0,) * len(shape))


def struct(shape, dtype):
    return jax.ShapeDtypeStruct(shape, dtype)


def round_pairs(count, k, back=False):
    pairs = []
    for i in range(count):
        row, seg, place = i // 8, (i % 8) // 4, i % 4
        pair = (i, row * 8 + 2 * ((place + k) % 4) + seg)
        pairs.append(pair[::-1] if back else pair)
    return pairs


def shift_pairs(count, by):
    return [(i, i + by) for i in range(count) if 0 <= i + by < count]


def pack(info, arrays, widths):
    rows = arrays[0].shape[0]
    total = sum(widths)

    def kernel(info_ref, *refs):
        ins, outs = refs[: len(arrays)], refs[len(arrays) :]
        for k in range(4):
            head = (info_ref[0] + k) & 3
            at = 0
            for ref, width in zip(ins, widths):
                first = pl.multiple_of(head * width, 128)
                outs[k][:, at : at + width] = ref[:, pl.ds(first, width)]
                at += width

    return pl.pallas_call(
        kernel,
        grid_spec=pltpu.PrefetchScalarGridSpec(
            num_scalar_prefetch=1,
            grid=(1,),
            in_specs=[whole(a.shape) for a in arrays],
            out_specs=[whole((rows, total))] * 4,
        ),
        out_shape=[struct((rows, total), BF)] * 4,
        cost_estimate=pl.CostEstimate(
            flops=0, bytes_accessed=2 * rows * total * 8, transcendentals=0
        ),
        name="pack",
    )(info, *arrays)


def positive(x):
    x = x.astype(F32)
    return jnp.where(x > 0, x + 1.0, jnp.exp(jnp.minimum(x, 0.0))).astype(BF)


def own_segment(info, parts):
    def kernel(info_ref, a, b, c, d, kv_ref, delta_ref):
        for k, ref in enumerate((a, b, c, d)):
            place = (info_ref[1] - k) & 3
            kv_ref[pl.ds(pl.multiple_of(place * BLK, BLK), BLK), :] = ref[...]
        total = jnp.zeros((HDIM, HDIM), F32)
        norm = jnp.zeros((1, HDIM), F32)
        for ref in (a, b, c, d):
            feat = positive(ref[:, :HDIM])
            total = total + lax.dot_general(
                feat, ref[:, HDIM:], (((0,), (0,)), ((), ())), preferred_element_type=F32
            )
            norm = norm + jnp.sum(feat.astype(F32), axis=0, keepdims=True)
        delta_ref[:HDIM, :] = total
        delta_ref[HDIM:, :] = jnp.broadcast_to(norm, (8, HDIM))

    return pl.pallas_call(
        kernel,
        grid_spec=pltpu.PrefetchScalarGridSpec(
            num_scalar_prefetch=1,
            grid=(1,),
            in_specs=[whole((BLK, 2 * HDIM))] * 4,
            out_specs=[whole((SEG, 2 * HDIM)), whole((HDIM + 8, HDIM))],
        ),
        out_shape=[struct((SEG, 2 * HDIM), BF), struct((HDIM + 8, HDIM), F32)],
        cost_estimate=pl.CostEstimate(
            flops=2 * SEG * HDIM * HDIM, bytes_accessed=4 * SEG * HDIM * 2, transcendentals=0
        ),
        name="own_segment",
    )(info, *parts)


def two_terms(x):
    high = x.astype(BF)
    return high, (x - high.astype(F32)).astype(BF)


def mixed_heads(info, gates, queries, own, two, four, near, swap, far, memory, first, count):
    rows = GROUP * count

    def kernel(info_ref, gate_ref, *refs):
        q_refs = refs[:4]
        own_ref, two_ref, four_ref, near_ref, swap_ref, far_ref, mem_ref = refs[4:11]
        out_refs = refs[11:15]
        k_all, v_all, q_now, o_now = refs[15:]
        step = pl.program_id(0)
        core, segment, head = info_ref[2], info_ref[3], info_ref[1]

        def place(age, ref):
            at = pl.ds((BACK - age) * SEG, SEG)
            k_all[at, :HDIM] = ref[:, :HDIM]
            v_all[at, :HDIM] = ref[:, HDIM:]

        @pl.when(step == 0)
        def _():
            place(0, own_ref)
            place(2, two_ref)
            place(4, four_ref)

            @pl.when(core == 0)
            def _():
                place(1, swap_ref)
                place(3, far_ref)

            @pl.when(core == 1)
            def _():
                place(1, near_ref)
                place(3, swap_ref)

            lane = lax.broadcasted_iota(jnp.int32, (SEG, HDIM), 1)
            for age in range(BACK + 1):
                bias = jnp.where(segment >= age, 0.0, -1e30).astype(F32)
                at = pl.ds((BACK - age) * SEG, SEG)
                k_all[at, HDIM:] = jnp.where(lane == 0, bias, 0.0).astype(BF)
            v_all[:, HDIM:] = jnp.ones((SPAN, HDIM), BF)

        for k in range(4):

            @pl.when(step == k)
            def _(k=k):
                q_now[...] = q_refs[k][first : first + count, :]

        base = pl.multiple_of(((head - step) & 3) * BLK + first, 64)
        q_bare = jnp.concatenate(
            [q_now[:, g * HDIM : (g + 1) * HDIM] for g in range(GROUP)], axis=0
        )
        lane = lax.broadcasted_iota(jnp.int32, (rows, HDIM), 1)
        q = jnp.concatenate([q_bare, jnp.where(lane == 0, 1.0, 0.0).astype(BF)], axis=1)

        def keys_at(offset, size):
            return k_all[pl.ds(pl.multiple_of(base + offset, 64), size), :]

        def values_at(offset, size):
            return v_all[pl.ds(pl.multiple_of(base + offset, 64), size), :]

        def scores(offset, size):
            return lax.dot_general(q, keys_at(offset, size), LAST, preferred_element_type=F32)

        def summed(p, offset, size):
            return jnp.dot(p, values_at(offset, size), preferred_element_type=F32)

        token = lax.broadcasted_iota(jnp.int32, (rows, count), 0) & (count - 1)
        newer = lax.broadcasted_iota(jnp.int32, (rows, count), 1) <= token
        s = jnp.where(newer, scores(WINDOW, count), scores(0, count))
        top = jnp.max(s, axis=1, keepdims=True)
        p = jnp.exp2((s - top) * SCALE)
        acc = summed(jnp.where(newer, p, 0.0).astype(BF), WINDOW, count)
        acc = acc + summed(jnp.where(newer, 0.0, p).astype(BF), 0, count)
        at = count
        while at < WINDOW:
            size = min(KEYS_STEP, WINDOW - at)
            s = scores(at, size)
            newest = jnp.maximum(top, jnp.max(s, axis=1, keepdims=True))
            p = jnp.exp2((s - newest) * SCALE).astype(BF)
            acc = acc * jnp.exp2((top - newest) * SCALE) + summed(p, at, size)
            top = newest
            at += size

        feat = positive(q_bare)
        mem_high, mem_low = two_terms(mem_ref[:HDIM, :])
        recalled = jnp.dot(feat, mem_high, preferred_element_type=F32)
        recalled = recalled + jnp.dot(feat, mem_low, preferred_element_type=F32)
        norm = jnp.broadcast_to(mem_ref[HDIM : HDIM + 1, :], (HDIM, HDIM))
        norm_high, norm_low = two_terms(norm)
        below = lax.dot_general(feat, norm_high, LAST, preferred_element_type=F32)
        below = below + lax.dot_general(feat, norm_low, LAST, preferred_element_type=F32)
        retrieved = recalled / (1.0 + below)
        local = acc[:, :HDIM] / acc[:, HDIM:]
        for g in range(GROUP):
            share = gate_ref[head * GROUP + g]
            at = slice(g * count, (g + 1) * count)
            value = share * retrieved[at] + (1.0 - share) * local[at]
            o_now[:, g * HDIM : (g + 1) * HDIM] = value.astype(BF)
        for k in range(4):

            @pl.when(step == k)
            def _(k=k):
                out_refs[k][...] = o_now[...]

    kv_spec = whole((SEG, 2 * HDIM))
    return pl.pallas_call(
        kernel,
        grid_spec=pltpu.PrefetchScalarGridSpec(
            num_scalar_prefetch=1,
            grid=(4,),
            in_specs=[pl.BlockSpec(memory_space=pltpu.SMEM)]
            + [whole((BLK, GROUP * HDIM))] * 4
            + [kv_spec] * 6
            + [whole((HDIM + 8, HDIM))],
            out_specs=[whole((count, GROUP * HDIM))] * 4,
            scratch_shapes=[
                pltpu.VMEM((SPAN, 2 * HDIM), BF),
                pltpu.VMEM((SPAN, 2 * HDIM), BF),
                pltpu.VMEM((count, GROUP * HDIM), BF),
                pltpu.VMEM((count, GROUP * HDIM), BF),
            ],
        ),
        out_shape=[struct((count, GROUP * HDIM), BF)] * 4,
        compiler_params=pltpu.CompilerParams(vmem_limit_bytes=40 * MB),
        cost_estimate=pl.CostEstimate(
            flops=16 * rows * WINDOW * HDIM * 4,
            bytes_accessed=4 * MB,
            transcendentals=4 * rows * WINDOW,
        ),
        name="mixed_heads",
    )(info, gates, *queries, own, two, four, near, swap, far, memory)


def projected(info, mixed, weight, side, dtype):
    count = mixed[0].shape[0]
    depth, width = weight.shape
    tile = 512
    tiles = width // 2 // tile

    def kernel(info_ref, a, b, c, d, w_ref, out_ref, held):
        @pl.when(pl.program_id(0) == 0)
        def _():
            for k, ref in enumerate((a, b, c, d)):
                head = (info_ref[0] + k) & 3
                at = pl.multiple_of(head * GROUP * HDIM, 128)
                held[:, pl.ds(at, GROUP * HDIM)] = ref[...]

        out_ref[...] = jnp.dot(held[...], w_ref[...], preferred_element_type=F32).astype(dtype)

    return pl.pallas_call(
        kernel,
        grid_spec=pltpu.PrefetchScalarGridSpec(
            num_scalar_prefetch=1,
            grid=(tiles,),
            in_specs=[whole((count, GROUP * HDIM))] * 4
            + [pl.BlockSpec((depth, tile), lambda n, info: (0, (info[4] ^ side) * tiles + n))],
            out_specs=pl.BlockSpec((count, tile), lambda n, info: (0, n)),
            scratch_shapes=[pltpu.VMEM((count, depth), BF)],
        ),
        out_shape=struct((count, width // 2), dtype),
        compiler_params=pltpu.CompilerParams(vmem_limit_bytes=24 * MB),
        cost_estimate=pl.CostEstimate(
            flops=2 * count * depth * width // 2, bytes_accessed=depth * width, transcendentals=0
        ),
        name="projected",
    )(info, *mixed, weight)


def per_device(queries, keys, values, gate_logit, out_weight):
    size = lax.axis_size("seq")
    seq = lax.axis_index("seq")
    side = lax.axis_index("head")
    row, core = seq // 8, seq % 2
    info = jnp.stack(
        [seq % 4, (seq % 8) // 2, core, 2 * row + core, side, row % 2]
    ).astype(jnp.int32)
    gates = jax.nn.sigmoid(gate_logit.astype(F32))

    def moved(value, pairs):
        return lax.ppermute(value, "seq", pairs)

    kv_out = pack(info, (keys, values), (HDIM, HDIM))
    kv_in = [moved(kv_out[k], round_pairs(size, k)) for k in range(4)]
    q_out = pack(info, (queries,), (GROUP * HDIM,))
    tied = lax.optimization_barrier((*kv_in, *q_out))
    kv_in, q_out = tied[:4], tied[4:]
    own, delta = own_segment(info, kv_in)
    two = moved(own, shift_pairs(size, 8))
    four = moved(own, shift_pairs(size, 16))
    near = moved(own, [(i, i + 1) for i in range(0, size, 2)])
    q_in = [moved(q_out[k], round_pairs(size, k)) for k in range(4)]

    other = moved(delta, [(i, i ^ 1) for i in range(size)])
    chip = delta + other
    flipped = moved(chip, [(i, i ^ 8) for i in range(size)])
    both = chip + flipped
    memory = jnp.where(core == 1, other, 0.0) + jnp.where(row % 2 == 1, flipped, 0.0)
    for step in range(1, size // 16):
        memory = memory + moved(both, shift_pairs(size, 16 * step))

    swap = moved(two, [(i, i ^ 1) for i in range(size)])
    far = moved(four, [(i + 1, i) for i in range(0, size, 2)])

    outs = []
    for first, count in CHUNKS:
        parts = mixed_heads(
            info, gates, q_in, own, two, four, near, swap, far, memory, first, count
        )
        parts = [moved(parts[k], round_pairs(size, k, back=True)) for k in range(4)]
        theirs = projected(info, parts, out_weight, 1, BF)
        arrived = lax.ppermute(theirs, "head", [(0, 1), (1, 0)])
        mine = projected(info, parts, out_weight, 0, F32)
        outs.append((mine, arrived))
    return jnp.concatenate([(m + a.astype(F32)).astype(BF) for m, a in outs], axis=0)


def solution(mesh):
    in_specs = (P("seq", "head"), P("seq", "head"), P("seq", "head"), P("head"), P("head", None))
    return jax.shard_map(
        per_device, mesh=mesh, in_specs=in_specs, out_specs=P("seq", "head"), check_vma=False
    )
```

```python
import functools
import math

import jax
import jax.numpy as jnp
from jax import lax
from jax.experimental import pallas as pl
from jax.experimental.pallas import tpu as pltpu
from jax.sharding import PartitionSpec as P

HDIM = 128
WINDOW = 4096
SEG = 1024
BLK = 256
GROUP = 4
ROW = 8 * BLK
BACK = WINDOW // ROW
SPAN = WINDOW + ROW
SCALE = math.log2(math.e) / math.sqrt(HDIM)
CHUNKS = ((0, 128), (128, 128))
KEYS_STEP = 512
EARLY = True
BF = jnp.bfloat16
F32 = jnp.float32
LAST = (((1,), (1,)), ((), ()))
MB = 1 << 20
MEM = HDIM + 8
TAIL = 96
REST = 3 * BLK + TAIL


def whole(shape):
    return pl.BlockSpec(shape, lambda *_: (0,) * len(shape))


def struct(shape, dtype):
    return jax.ShapeDtypeStruct(shape, dtype)


def across(count, by):
    return [(i, (i // 8) * 8 + (i + 2 * by) % 8) for i in range(count)]


def shift_pairs(count, by):
    return [(i, i + by) for i in range(count) if 0 <= i + by < count]


def core_pairs(count):
    return [(i, i ^ 1) for i in range(count)]


def chip_index():
    return lax.rem(lax.axis_index("seq"), 8) // 2


def pack(arrays, widths):
    rows = arrays[0].shape[0]
    total = sum(widths)
    count = len(arrays)

    def kernel(*refs):
        ins, outs = refs[:count], refs[count:]
        for k in range(4):
            head = (chip_index() + k) & 3
            at = 0
            for ref, width in zip(ins, widths):
                first = pl.multiple_of(head * width, 128)
                outs[k][:, at : at + width] = ref[:, pl.ds(first, width)]
                at += width

    return pl.pallas_call(
        kernel,
        out_shape=[struct((rows, total), BF)] * 4,
        cost_estimate=pl.CostEstimate(
            flops=0, bytes_accessed=2 * rows * total * 8, transcendentals=0
        ),
        compiler_params=pltpu.CompilerParams(vmem_limit_bytes=12 * MB),
        name="pack",
    )(*arrays)


def positive(x):
    x = x.astype(F32)
    return jnp.where(x > 0, x + 1.0, jnp.exp(jnp.minimum(x, 0.0))).astype(BF)


def two_terms(x):
    high = x.astype(BF)
    return high, (x - high.astype(F32)).astype(BF)


def with_deltas(parts):
    def kernel(*refs):
        out, first_ref = refs[4:]
        sums = [jnp.zeros((HDIM, HDIM), F32) for _ in range(2)]
        norms = [jnp.zeros((1, HDIM), F32) for _ in range(2)]
        for k in range(4):
            block = refs[k][...]
            if k:
                out[(k - 1) * BLK : k * BLK, :] = block
            feat = positive(block[:, :HDIM])
            product = lax.dot_general(
                feat, block[:, HDIM:], (((0,), (0,)), ((), ())), preferred_element_type=F32
            )
            norm = jnp.sum(feat.astype(F32), axis=0, keepdims=True)
            half = ((chip_index() - k) & 3) // 2
            for n in range(2):
                sums[n] = sums[n] + jnp.where(half == n, product, 0.0)
                norms[n] = norms[n] + jnp.where(half == n, norm, 0.0)
        total = (sums[0] + sums[1]).astype(BF)
        at, half = 3 * BLK, HDIM // 2
        out[at : at + half, :HDIM] = total[:half]
        out[at : at + half, HDIM:] = total[half:]
        high, low = two_terms(jnp.broadcast_to(norms[0] + norms[1], (REST - at - half, HDIM)))
        out[at + half :, :HDIM] = high
        out[at + half :, HDIM:] = low
        first_ref[:HDIM, :] = sums[0]
        first_ref[HDIM:, :] = jnp.broadcast_to(norms[0], (MEM - HDIM, HDIM))

    return pl.pallas_call(
        kernel,
        out_shape=[struct((REST, 2 * HDIM), BF), struct((MEM, HDIM), F32)],
        cost_estimate=pl.CostEstimate(
            flops=2 * SEG * HDIM * HDIM, bytes_accessed=8 * SEG * HDIM * 2, transcendentals=0
        ),
        compiler_params=pltpu.CompilerParams(vmem_limit_bytes=12 * MB),
        name="with_deltas",
    )(*parts)


def near_sums(rests, firsts):
    half = HDIM // 2

    def kernel(*refs):
        first_refs, (three_ref, near_ref) = refs[6:8], refs[8:]

        def delta(age):
            memory = jnp.zeros((HDIM, HDIM), F32)
            norm = jnp.zeros((MEM - HDIM, HDIM), F32)
            for ref in (refs[age], refs[3 + age]):
                value = ref[:half, :].astype(F32)
                memory = memory + jnp.concatenate([value[:, :HDIM], value[:, HDIM:]], axis=0)
                value = ref[half : half + 8, :].astype(F32)
                norm = norm + (value[:, :HDIM] + value[:, HDIM:])
            return jnp.concatenate([memory, norm], axis=0)

        before = delta(1) + delta(2)
        near_ref[0] = before
        near_ref[1] = before + (first_refs[0][...] + first_refs[1][...])
        three_ref[...] = before + delta(0)

    spec = pl.BlockSpec((TAIL, 2 * HDIM), lambda i: (3 * BLK // TAIL, 0))
    return pl.pallas_call(
        kernel,
        grid=(1,),
        in_specs=[spec] * 6 + [whole((MEM, HDIM))] * 2,
        out_specs=[whole((MEM, HDIM)), whole((2, MEM, HDIM))],
        out_shape=[struct((MEM, HDIM), F32), struct((2, MEM, HDIM), F32)],
        cost_estimate=pl.CostEstimate(flops=0, bytes_accessed=2 * MB, transcendentals=0),
        compiler_params=pltpu.CompilerParams(vmem_limit_bytes=12 * MB),
        name="near_sums",
    )(*rests, *firsts)


def mixed_heads(info, gates, queries, rows_mine, rows_other, memory, first, count, rounds):
    rows = GROUP * count
    number = len(rounds)
    lowest = rounds[0]

    def kernel(info_ref, gate_ref, *refs):
        q_refs, refs = refs[:number], refs[number:]
        mine_refs, other_refs, refs = refs[:6], refs[6:12], refs[12:]
        near_ref, far_refs, refs = refs[0], refs[1:3], refs[3:]
        out_refs = refs[:number]
        k_all, v_all, q_now, o_now = refs[number:]
        step = pl.program_id(0)
        chip, core, row = info_ref[0], info_ref[1], info_ref[2]
        source = (chip - step - lowest) & 3

        @pl.when(step == 0)
        def _():
            lane = lax.broadcasted_iota(jnp.int32, (ROW, HDIM), 1)
            for age in range(BACK + 1):
                for k in range(4):
                    block = slice(0, BLK) if k == 0 else slice((k - 1) * BLK, k * BLK)
                    for refs, c in ((mine_refs, core), (other_refs, 1 - core)):
                        ref = refs[2 * age + (k > 0)]
                        place = 2 * ((chip - k) & 3) + c
                        at = pl.multiple_of((BACK - age) * ROW + place * BLK, BLK)
                        k_all[pl.ds(at, BLK), :HDIM] = ref[block, :HDIM]
                        v_all[pl.ds(at, BLK), :HDIM] = ref[block, HDIM:]
                bias = jnp.where(row >= age, 0.0, -1e30).astype(F32)
                at = pl.ds((BACK - age) * ROW, ROW)
                k_all[at, HDIM:] = jnp.where(lane == 0, bias, 0.0).astype(BF)
            v_all[:, HDIM:] = jnp.ones((SPAN, HDIM), BF)

        for k in range(number):

            @pl.when(step == k)
            def _(k=k):
                q_now[...] = q_refs[k][first : first + count, :]

        base = pl.multiple_of((2 * source + core) * BLK + first, 64)
        q_bare = jnp.concatenate(
            [q_now[:, g * HDIM : (g + 1) * HDIM] for g in range(GROUP)], axis=0
        )
        lane = lax.broadcasted_iota(jnp.int32, (rows, HDIM), 1)
        q = jnp.concatenate([q_bare, jnp.where(lane == 0, 1.0, 0.0).astype(BF)], axis=1)

        def keys_at(offset, size):
            return k_all[pl.ds(pl.multiple_of(base + offset, 64), size), :]

        def values_at(offset, size):
            return v_all[pl.ds(pl.multiple_of(base + offset, 64), size), :]

        def scores(offset, size):
            return lax.dot_general(q, keys_at(offset, size), LAST, preferred_element_type=F32)

        def summed(p, offset, size):
            return jnp.dot(p, values_at(offset, size), preferred_element_type=F32)

        token = lax.broadcasted_iota(jnp.int32, (rows, count), 0) & (count - 1)
        newer = lax.broadcasted_iota(jnp.int32, (rows, count), 1) <= token
        s = jnp.where(newer, scores(WINDOW, count), scores(0, count))
        top = jnp.max(s, axis=1, keepdims=True)
        p = jnp.exp2((s - top) * SCALE)
        acc = summed(jnp.where(newer, p, 0.0).astype(BF), WINDOW, count)
        acc = acc + summed(jnp.where(newer, 0.0, p).astype(BF), 0, count)
        at = count
        while at < WINDOW:
            size = min(KEYS_STEP, WINDOW - at)
            s = scores(at, size)
            newest = jnp.maximum(top, jnp.max(s, axis=1, keepdims=True))
            p = jnp.exp2((s - newest) * SCALE).astype(BF)
            acc = acc * jnp.exp2((top - newest) * SCALE) + summed(p, at, size)
            top = newest
            at += size

        feat = positive(q_bare)
        half = source // 2
        known = near_ref[half] + far_refs[0][...] + far_refs[1][...]
        mem_high, mem_low = two_terms(known[:HDIM])
        recalled = jnp.dot(feat, mem_high, preferred_element_type=F32)
        recalled = recalled + jnp.dot(feat, mem_low, preferred_element_type=F32)
        norm = jnp.broadcast_to(known[HDIM : HDIM + 1], (HDIM, HDIM))
        norm_high, norm_low = two_terms(norm)
        below = lax.dot_general(feat, norm_high, LAST, preferred_element_type=F32)
        below = below + lax.dot_general(feat, norm_low, LAST, preferred_element_type=F32)
        retrieved = recalled / (1.0 + below)
        local = acc[:, :HDIM] / acc[:, HDIM:]
        for g in range(GROUP):
            share = gate_ref[chip * GROUP + g]
            at = slice(g * count, (g + 1) * count)
            value = share * retrieved[at] + (1.0 - share) * local[at]
            o_now[:, g * HDIM : (g + 1) * HDIM] = value.astype(BF)
        for k in range(number):

            @pl.when(step == k)
            def _(k=k):
                out_refs[k][...] = o_now[...]

    kv_specs = [whole((BLK, 2 * HDIM)), whole((REST, 2 * HDIM))] * 6
    return pl.pallas_call(
        kernel,
        grid_spec=pltpu.PrefetchScalarGridSpec(
            num_scalar_prefetch=1,
            grid=(number,),
            in_specs=[pl.BlockSpec(memory_space=pltpu.SMEM)]
            + [whole((BLK, GROUP * HDIM))] * number
            + kv_specs
            + [whole((2, MEM, HDIM)), whole((MEM, HDIM)), whole((MEM, HDIM))],
            out_specs=[whole((count, GROUP * HDIM))] * number,
            scratch_shapes=[
                pltpu.VMEM((SPAN, 2 * HDIM), BF),
                pltpu.VMEM((SPAN, 2 * HDIM), BF),
                pltpu.VMEM((count, GROUP * HDIM), BF),
                pltpu.VMEM((count, GROUP * HDIM), BF),
            ],
        ),
        out_shape=[struct((count, GROUP * HDIM), BF)] * number,
        compiler_params=pltpu.CompilerParams(vmem_limit_bytes=40 * MB),
        cost_estimate=pl.CostEstimate(
            flops=4 * number * rows * WINDOW * HDIM * 4,
            bytes_accessed=4 * MB,
            transcendentals=number * rows * WINDOW,
        ),
        name="mixed_heads",
    )(info, gates, *[queries[k] for k in rounds], *rows_mine, *rows_other, *memory)


def projected(info, mixed, weight, side, dtype):
    count = mixed[0].shape[0]
    depth, width = weight.shape
    tile = 512
    tiles = width // 2 // tile

    def kernel(info_ref, a, b, c, d, w_ref, out_ref, held):
        @pl.when(pl.program_id(0) == 0)
        def _():
            for k, ref in enumerate((a, b, c, d)):
                head = (info_ref[0] + k) & 3
                at = pl.multiple_of(head * GROUP * HDIM, 128)
                held[:, pl.ds(at, GROUP * HDIM)] = ref[...]

        out_ref[...] = jnp.dot(held[...], w_ref[...], preferred_element_type=F32).astype(dtype)

    return pl.pallas_call(
        kernel,
        grid_spec=pltpu.PrefetchScalarGridSpec(
            num_scalar_prefetch=1,
            grid=(tiles,),
            in_specs=[whole((count, GROUP * HDIM))] * 4
            + [pl.BlockSpec((depth, tile), lambda n, info: (0, (info[3] ^ side) * tiles + n))],
            out_specs=pl.BlockSpec((count, tile), lambda n, info: (0, n)),
            scratch_shapes=[pltpu.VMEM((count, depth), BF)],
        ),
        out_shape=struct((count, width // 2), dtype),
        compiler_params=pltpu.CompilerParams(vmem_limit_bytes=24 * MB),
        cost_estimate=pl.CostEstimate(
            flops=2 * count * depth * width // 2, bytes_accessed=depth * width, transcendentals=0
        ),
        name="projected",
    )(info, *mixed, weight)


def per_device(queries, keys, values, gate_logit, out_weight):
    size = lax.axis_size("seq")
    seq = lax.axis_index("seq")
    side = lax.axis_index("head")
    row, core = seq // 8, seq % 2
    info = jnp.stack([(seq % 8) // 2, core, row, side]).astype(jnp.int32)
    gates = jax.nn.sigmoid(gate_logit.astype(F32))

    def moved(value, pairs):
        return lax.ppermute(value, "seq", pairs)

    def to_chips(parts, sign):
        return [parts[0]] + [moved(parts[k], across(size, sign * k)) for k in (1, 2, 3)]

    kv_out = pack((keys, values), (HDIM, HDIM))
    kv_in = to_chips(kv_out, 1)
    q_out = pack((queries,), (GROUP * HDIM,))
    if EARLY:
        early = [moved(kv_out[0], shift_pairs(size, 8 * by)) for by in (1, 2)]
        tied = lax.optimization_barrier((*kv_in, *early, *q_out))
        kv_in, early, q_out = tied[:4], tied[4:6], tied[6:]
    else:
        tied = lax.optimization_barrier((*kv_in, *q_out))
        kv_in, q_out = tied[:4], tied[4:]
        early = [moved(kv_in[0], shift_pairs(size, 8 * by)) for by in (1, 2)]
    rest, first = with_deltas(kv_in)
    own = (kv_in[0], rest)
    last = (early[0], moved(own[1], shift_pairs(size, 8)))
    older = (early[1], moved(own[1], shift_pairs(size, 16)))
    q_in = to_chips(q_out, 1)
    tied = lax.optimization_barrier((*last, *older, *q_in[1:]))
    last, older, q_in[1:] = tied[:2], tied[2:4], tied[4:]

    mine = (*own, *last, *older)
    other = tuple(moved(v, core_pairs(size)) for v in mine)
    three, near = near_sums(
        (*mine[1::2], *other[1::2]), [first, moved(first, core_pairs(size))]
    )
    memory = (near, moved(three, shift_pairs(size, 24)), moved(three, shift_pairs(size, 48)))

    def heads(which, chunk, rounds):
        first, count = CHUNKS[chunk]
        return mixed_heads(info, gates, which, mine, other, memory, first, count, rounds)

    def back(part, k):
        return moved(part, across(size, -k)) if k else part

    def swapped(value):
        return lax.ppermute(value, "head", [(0, 1), (1, 0)])

    zero, one, two, three = heads(q_in, 0, (0, 1, 2, 3))
    parts = [zero, back(one, 1), back(two, 2), back(three, 3)]
    ahead = heads(q_in, 1, (1, 2, 3))
    tied = lax.optimization_barrier((*parts, *ahead))
    parts, ahead = tied[:4], tied[4:]
    theirs = projected(info, parts, out_weight, 1, BF)
    theirs, q_self = lax.optimization_barrier((theirs, q_in[0]))
    arrived = swapped(theirs)
    later = [back(ahead[k - 1], k) for k in (1, 2, 3)]
    later = [*heads([q_self], 1, (0,)), *later]
    theirs_later = projected(info, later, out_weight, 1, BF)
    arrived_later = swapped(theirs_later)
    first = projected(info, parts, out_weight, 0, F32) + arrived.astype(F32)
    second = projected(info, later, out_weight, 0, F32) + arrived_later.astype(F32)
    return jnp.concatenate([first.astype(BF), second.astype(BF)], axis=0)


def solution(mesh):
    in_specs = (P("seq", "head"), P("seq", "head"), P("seq", "head"), P("head"), P("head", None))
    return jax.shard_map(
        per_device, mesh=mesh, in_specs=in_specs, out_specs=P("seq", "head"), check_vma=False
    )
```

```python
import functools
import math

import jax
import jax.numpy as jnp
from jax import lax
from jax.experimental import pallas as pl
from jax.experimental.pallas import tpu as pltpu
from jax.sharding import PartitionSpec as P

HDIM = 128
WINDOW = 4096
SEG = 1024
BLK = 256
GROUP = 4
ROW = 8 * BLK
BACK = WINDOW // ROW
SPAN = WINDOW + ROW
SCALE = math.log2(math.e) / math.sqrt(HDIM)
CHUNKS = ((0, 128), (128, 128))
KEYS_STEP = 512
EARLY = True
BF = jnp.bfloat16
F32 = jnp.float32
LAST = (((1,), (1,)), ((), ()))
MB = 1 << 20
MEM = HDIM + 8
TAIL = 96
REST = 3 * BLK + TAIL


def whole(shape):
    return pl.BlockSpec(shape, lambda *_: (0,) * len(shape))


def struct(shape, dtype):
    return jax.ShapeDtypeStruct(shape, dtype)


def across(count, by):
    return [(i, (i // 8) * 8 + (i + 2 * by) % 8) for i in range(count)]


def shift_pairs(count, by):
    return [(i, i + by) for i in range(count) if 0 <= i + by < count]


def core_pairs(count):
    return [(i, i ^ 1) for i in range(count)]


def chip_index():
    return lax.rem(lax.axis_index("seq"), 8) // 2


def pack(arrays, widths):
    rows = arrays[0].shape[0]
    total = sum(widths)
    count = len(arrays)

    def kernel(*refs):
        ins, outs = refs[:count], refs[count:]
        for k in range(4):
            head = (chip_index() + k) & 3
            at = 0
            for ref, width in zip(ins, widths):
                first = pl.multiple_of(head * width, 128)
                outs[k][:, at : at + width] = ref[:, pl.ds(first, width)]
                at += width

    return pl.pallas_call(
        kernel,
        out_shape=[struct((rows, total), BF)] * 4,
        cost_estimate=pl.CostEstimate(
            flops=0, bytes_accessed=2 * rows * total * 8, transcendentals=0
        ),
        compiler_params=pltpu.CompilerParams(vmem_limit_bytes=12 * MB),
        name="pack",
    )(*arrays)


def positive(x):
    x = x.astype(F32)
    return jnp.where(x > 0, x + 1.0, jnp.exp(jnp.minimum(x, 0.0))).astype(BF)


def two_terms(x):
    high = x.astype(BF)
    return high, (x - high.astype(F32)).astype(BF)


def with_deltas(parts):
    def kernel(*refs):
        out, first_ref = refs[4:]
        sums = [jnp.zeros((HDIM, HDIM), F32) for _ in range(2)]
        norms = [jnp.zeros((1, HDIM), F32) for _ in range(2)]
        for k in range(4):
            block = refs[k][...]
            if k:
                out[(k - 1) * BLK : k * BLK, :] = block
            feat = positive(block[:, :HDIM])
            product = lax.dot_general(
                feat, block[:, HDIM:], (((0,), (0,)), ((), ())), preferred_element_type=F32
            )
            norm = jnp.sum(feat.astype(F32), axis=0, keepdims=True)
            half = ((chip_index() - k) & 3) // 2
            for n in range(2):
                sums[n] = sums[n] + jnp.where(half == n, product, 0.0)
                norms[n] = norms[n] + jnp.where(half == n, norm, 0.0)
        total = (sums[0] + sums[1]).astype(BF)
        at, half = 3 * BLK, HDIM // 2
        out[at : at + half, :HDIM] = total[:half]
        out[at : at + half, HDIM:] = total[half:]
        high, low = two_terms(jnp.broadcast_to(norms[0] + norms[1], (REST - at - half, HDIM)))
        out[at + half :, :HDIM] = high
        out[at + half :, HDIM:] = low
        first_ref[:HDIM, :] = sums[0]
        first_ref[HDIM:, :] = jnp.broadcast_to(norms[0], (MEM - HDIM, HDIM))

    return pl.pallas_call(
        kernel,
        out_shape=[struct((REST, 2 * HDIM), BF), struct((MEM, HDIM), F32)],
        cost_estimate=pl.CostEstimate(
            flops=2 * SEG * HDIM * HDIM, bytes_accessed=8 * SEG * HDIM * 2, transcendentals=0
        ),
        compiler_params=pltpu.CompilerParams(vmem_limit_bytes=12 * MB),
        name="with_deltas",
    )(*parts)


def near_sums(rests, firsts):
    half = HDIM // 2

    def kernel(*refs):
        first_refs, (three_ref, near_ref) = refs[6:8], refs[8:]

        def delta(age):
            memory = jnp.zeros((HDIM, HDIM), F32)
            norm = jnp.zeros((MEM - HDIM, HDIM), F32)
            for ref in (refs[age], refs[3 + age]):
                value = ref[:half, :].astype(F32)
                memory = memory + jnp.concatenate([value[:, :HDIM], value[:, HDIM:]], axis=0)
                value = ref[half : half + 8, :].astype(F32)
                norm = norm + (value[:, :HDIM] + value[:, HDIM:])
            return jnp.concatenate([memory, norm], axis=0)

        before = delta(1) + delta(2)
        near_ref[0] = before
        near_ref[1] = before + (first_refs[0][...] + first_refs[1][...])
        three_ref[...] = before + delta(0)

    spec = pl.BlockSpec((TAIL, 2 * HDIM), lambda i: (3 * BLK // TAIL, 0))
    return pl.pallas_call(
        kernel,
        grid=(1,),
        in_specs=[spec] * 6 + [whole((MEM, HDIM))] * 2,
        out_specs=[whole((MEM, HDIM)), whole((2, MEM, HDIM))],
        out_shape=[struct((MEM, HDIM), F32), struct((2, MEM, HDIM), F32)],
        cost_estimate=pl.CostEstimate(flops=0, bytes_accessed=2 * MB, transcendentals=0),
        compiler_params=pltpu.CompilerParams(vmem_limit_bytes=12 * MB),
        name="near_sums",
    )(*rests, *firsts)


def in_order(info, rows_mine, rows_other):
    def kernel(info_ref, *refs):
        mine_refs, other_refs, (k_all, v_all) = refs[:6], refs[6:12], refs[12:]
        chip, core, row = info_ref[0], info_ref[1], info_ref[2]
        lane = lax.broadcasted_iota(jnp.int32, (ROW, HDIM), 1)
        for age in range(BACK + 1):
            for k in range(4):
                block = slice(0, BLK) if k == 0 else slice((k - 1) * BLK, k * BLK)
                for part, c in ((mine_refs, core), (other_refs, 1 - core)):
                    ref = part[2 * age + (k > 0)]
                    place = 2 * ((chip - k) & 3) + c
                    at = pl.multiple_of((BACK - age) * ROW + place * BLK, BLK)
                    k_all[pl.ds(at, BLK), :HDIM] = ref[block, :HDIM]
                    v_all[pl.ds(at, BLK), :HDIM] = ref[block, HDIM:]
            bias = jnp.where(row >= age, 0.0, -1e30).astype(F32)
            at = pl.ds((BACK - age) * ROW, ROW)
            k_all[at, HDIM:] = jnp.where(lane == 0, bias, 0.0).astype(BF)
        v_all[:, HDIM:] = jnp.ones((SPAN, HDIM), BF)

    return pl.pallas_call(
        kernel,
        grid_spec=pltpu.PrefetchScalarGridSpec(
            num_scalar_prefetch=1,
            grid=(1,),
            in_specs=[whole(v.shape) for v in (*rows_mine, *rows_other)],
            out_specs=[whole((SPAN, 2 * HDIM))] * 2,
        ),
        out_shape=[struct((SPAN, 2 * HDIM), BF)] * 2,
        compiler_params=pltpu.CompilerParams(vmem_limit_bytes=24 * MB),
        cost_estimate=pl.CostEstimate(flops=0, bytes_accessed=9 * MB, transcendentals=0),
        name="in_order",
    )(info, *rows_mine, *rows_other)


def mixed_heads(info, gates, queries, both, memory, first, count, rounds, given=None):
    rows = GROUP * count
    number = len(rounds)
    lowest = rounds[0]

    def kernel(info_ref, gate_ref, *refs):
        q_refs, refs = refs[:number], refs[number:]
        k_all, v_all, refs = refs[0], refs[1], refs[2:]
        if memory:
            near_ref, far_refs, refs = refs[0], refs[1:3], refs[3:]
        if given is not None:
            given_ref, refs = refs[0], refs[1:]
        out_refs = refs[:number]
        q_now, o_now, local_now = refs[number:]
        step = pl.program_id(0)
        chip, core = info_ref[0], info_ref[1]
        source = (chip - step - lowest) & 3

        for k in range(number):

            @pl.when(step == k)
            def _(k=k):
                q_now[...] = q_refs[k][first : first + count, :]

        base = pl.multiple_of((2 * source + core) * BLK + first, 64)
        q_bare = jnp.concatenate(
            [q_now[:, g * HDIM : (g + 1) * HDIM] for g in range(GROUP)], axis=0
        )
        lane = lax.broadcasted_iota(jnp.int32, (rows, HDIM), 1)
        q = jnp.concatenate([q_bare, jnp.where(lane == 0, 1.0, 0.0).astype(BF)], axis=1)

        def keys_at(offset, size):
            return k_all[pl.ds(pl.multiple_of(base + offset, 64), size), :]

        def values_at(offset, size):
            return v_all[pl.ds(pl.multiple_of(base + offset, 64), size), :]

        def scores(offset, size):
            return lax.dot_general(q, keys_at(offset, size), LAST, preferred_element_type=F32)

        def summed(p, offset, size):
            return jnp.dot(p, values_at(offset, size), preferred_element_type=F32)

        def attended():
            token = lax.broadcasted_iota(jnp.int32, (rows, count), 0) & (count - 1)
            newer = lax.broadcasted_iota(jnp.int32, (rows, count), 1) <= token
            k_ends = jnp.concatenate([keys_at(0, count), keys_at(WINDOW, count)], axis=0)
            v_ends = jnp.concatenate([values_at(0, count), values_at(WINDOW, count)], axis=0)
            s = lax.dot_general(q, k_ends, LAST, preferred_element_type=F32)
            s = jnp.where(newer, s[:, count:], s[:, :count])
            top = jnp.max(s, axis=1, keepdims=True)
            p = jnp.exp2((s - top) * SCALE)
            p = jnp.concatenate([jnp.where(newer, 0.0, p), jnp.where(newer, p, 0.0)], axis=1)
            acc = jnp.dot(p.astype(BF), v_ends, preferred_element_type=F32)
            at = count
            while at < WINDOW:
                size = min(KEYS_STEP, WINDOW - at)
                s = scores(at, size)
                newest = jnp.maximum(top, jnp.max(s, axis=1, keepdims=True))
                p = jnp.exp2((s - newest) * SCALE).astype(BF)
                acc = acc * jnp.exp2((top - newest) * SCALE) + summed(p, at, size)
                top = newest
                at += size
            return acc[:, :HDIM] / acc[:, HDIM:]

        if not memory:
            out_refs[0][...] = attended()
            return
        if given is None:
            local = attended()
        else:

            @pl.when(step == 0)
            def _():
                local_now[...] = given_ref[...]

            @pl.when(step != 0)
            def _():
                local_now[...] = attended()

            local = local_now[...]

        feat = positive(q_bare)
        half = source // 2
        known = near_ref[half] + far_refs[0][...] + far_refs[1][...]
        mem_high, mem_low = two_terms(known[:HDIM])
        recalled = jnp.dot(feat, mem_high, preferred_element_type=F32)
        recalled = recalled + jnp.dot(feat, mem_low, preferred_element_type=F32)
        norm = jnp.broadcast_to(known[HDIM : HDIM + 1], (HDIM, HDIM))
        norm_high, norm_low = two_terms(norm)
        below = lax.dot_general(feat, norm_high, LAST, preferred_element_type=F32)
        below = below + lax.dot_general(feat, norm_low, LAST, preferred_element_type=F32)
        retrieved = recalled / (1.0 + below)
        for g in range(GROUP):
            share = gate_ref[chip * GROUP + g]
            at = slice(g * count, (g + 1) * count)
            value = share * retrieved[at] + (1.0 - share) * local[at]
            o_now[:, g * HDIM : (g + 1) * HDIM] = value.astype(BF)
        for k in range(number):

            @pl.when(step == k)
            def _(k=k):
                out_refs[k][...] = o_now[...]

    extra = [*memory] + ([given] if given is not None else [])
    out = struct((count, GROUP * HDIM), BF) if memory else struct((rows, HDIM), F32)
    return pl.pallas_call(
        kernel,
        grid_spec=pltpu.PrefetchScalarGridSpec(
            num_scalar_prefetch=1,
            grid=(number,),
            in_specs=[pl.BlockSpec(memory_space=pltpu.SMEM)]
            + [whole((BLK, GROUP * HDIM))] * number
            + [whole((SPAN, 2 * HDIM))] * 2
            + [whole(a.shape) for a in extra],
            out_specs=[whole(out.shape)] * number,
            scratch_shapes=[
                pltpu.VMEM((count, GROUP * HDIM), BF),
                pltpu.VMEM((count, GROUP * HDIM), BF),
                pltpu.VMEM((rows, HDIM), F32),
            ],
        ),
        out_shape=[out] * number,
        compiler_params=pltpu.CompilerParams(vmem_limit_bytes=28 * MB),
        cost_estimate=pl.CostEstimate(
            flops=4 * number * rows * WINDOW * HDIM * 4,
            bytes_accessed=4 * MB,
            transcendentals=number * rows * WINDOW,
        ),
        name="mixed_heads",
    )(info, gates, *[queries[k] for k in rounds], *both, *extra)


def projected(info, mixed, weight, side, dtype):
    count = mixed[0].shape[0]
    depth, width = weight.shape
    tile = 512
    tiles = width // 2 // tile

    def kernel(info_ref, a, b, c, d, w_ref, out_ref, held):
        @pl.when(pl.program_id(0) == 0)
        def _():
            for k, ref in enumerate((a, b, c, d)):
                head = (info_ref[0] + k) & 3
                at = pl.multiple_of(head * GROUP * HDIM, 128)
                held[:, pl.ds(at, GROUP * HDIM)] = ref[...]

        out_ref[...] = jnp.dot(held[...], w_ref[...], preferred_element_type=F32).astype(dtype)

    return pl.pallas_call(
        kernel,
        grid_spec=pltpu.PrefetchScalarGridSpec(
            num_scalar_prefetch=1,
            grid=(tiles,),
            in_specs=[whole((count, GROUP * HDIM))] * 4
            + [pl.BlockSpec((depth, tile), lambda n, info: (0, (info[3] ^ side) * tiles + n))],
            out_specs=pl.BlockSpec((count, tile), lambda n, info: (0, n)),
            scratch_shapes=[pltpu.VMEM((count, depth), BF)],
        ),
        out_shape=struct((count, width // 2), dtype),
        compiler_params=pltpu.CompilerParams(vmem_limit_bytes=24 * MB),
        cost_estimate=pl.CostEstimate(
            flops=2 * count * depth * width // 2, bytes_accessed=depth * width, transcendentals=0
        ),
        name="projected",
    )(info, *mixed, weight)


def per_device(queries, keys, values, gate_logit, out_weight):
    size = lax.axis_size("seq")
    seq = lax.axis_index("seq")
    side = lax.axis_index("head")
    row, core = seq // 8, seq % 2
    info = jnp.stack([(seq % 8) // 2, core, row, side]).astype(jnp.int32)
    gates = jax.nn.sigmoid(gate_logit.astype(F32))

    def moved(value, pairs):
        return lax.ppermute(value, "seq", pairs)

    def to_chips(parts, sign):
        return [parts[0]] + [moved(parts[k], across(size, sign * k)) for k in (1, 2, 3)]

    kv_out = pack((keys, values), (HDIM, HDIM))
    kv_in = to_chips(kv_out, 1)
    q_out = pack((queries,), (GROUP * HDIM,))
    if EARLY:
        early = [moved(kv_out[0], shift_pairs(size, 8 * by)) for by in (1, 2)]
        tied = lax.optimization_barrier((*kv_in, *early, *q_out))
        kv_in, early, q_out = tied[:4], tied[4:6], tied[6:]
    else:
        tied = lax.optimization_barrier((*kv_in, *q_out))
        kv_in, q_out = tied[:4], tied[4:]
        early = [moved(kv_in[0], shift_pairs(size, 8 * by)) for by in (1, 2)]
    rest, first = with_deltas(kv_in)
    own = (kv_in[0], rest)
    last = (early[0], moved(own[1], shift_pairs(size, 8)))
    older = (early[1], moved(own[1], shift_pairs(size, 16)))
    q_in = to_chips(q_out, 1)
    tied = lax.optimization_barrier((*last, *older, *q_in[1:]))
    last, older, q_in[1:] = tied[:2], tied[2:4], tied[4:]

    mine = (*own, *last, *older)
    other = tuple(moved(v, core_pairs(size)) for v in mine)
    three, near = near_sums(
        (*mine[1::2], *other[1::2]), [first, moved(first, core_pairs(size))]
    )
    both = in_order(info, mine, other)
    memory = (near, moved(three, shift_pairs(size, 24)), moved(three, shift_pairs(size, 48)))

    def heads(which, chunk, rounds, memory, given=None):
        first, count = CHUNKS[chunk]
        return mixed_heads(
            info, gates, which, both, memory, first, count, rounds, given
        )

    def back(part, k):
        return moved(part, across(size, -k)) if k else part

    def swapped(value):
        return lax.ppermute(value, "head", [(0, 1), (1, 0)])

    zero, one, two, three = heads(q_in, 0, (0, 1, 2, 3), memory)
    parts = [zero, back(one, 1), back(two, 2), back(three, 3)]
    ahead = heads(q_in, 1, (1, 2, 3), memory)
    tied = lax.optimization_barrier((*parts, *ahead))
    parts, ahead = tied[:4], tied[4:]
    theirs = projected(info, parts, out_weight, 1, BF)
    theirs, q_self = lax.optimization_barrier((theirs, q_in[0]))
    later = [back(ahead[k - 1], k) for k in (1, 2, 3)]
    arrived = swapped(theirs)
    later = [*heads([q_self], 1, (0,), memory), *later]
    theirs_later = projected(info, later, out_weight, 1, BF)
    arrived_later = swapped(theirs_later)
    tied = lax.optimization_barrier((*parts, theirs_later))
    first = projected(info, tied[:4], out_weight, 0, F32) + arrived.astype(F32)
    second = projected(info, later, out_weight, 0, F32) + arrived_later.astype(F32)
    return jnp.concatenate([first.astype(BF), second.astype(BF)], axis=0)


def solution(mesh):
    in_specs = (P("seq", "head"), P("seq", "head"), P("seq", "head"), P("head"), P("head", None))
    return jax.shard_map(
        per_device, mesh=mesh, in_specs=in_specs, out_specs=P("seq", "head"), check_vma=False
    )
```

```python
import functools
import math

import jax
import jax.numpy as jnp
from jax import lax
from jax.experimental import pallas as pl
from jax.experimental.pallas import tpu as pltpu
from jax.sharding import PartitionSpec as P

HDIM = 128
WINDOW = 4096
SEG = 1024
BLK = 256
GROUP = 4
ROW = 8 * BLK
BACK = WINDOW // ROW
SPAN = WINDOW + ROW
SCALE = math.log2(math.e) / math.sqrt(HDIM)
CHUNKS = ((0, 128), (128, 128))
KEYS_STEP = 512
EARLY = True
BF = jnp.bfloat16
F32 = jnp.float32
LAST = (((1,), (1,)), ((), ()))
MB = 1 << 20
MEM = HDIM + 8
TAIL = 96
REST = 3 * BLK + TAIL


def whole(shape):
    return pl.BlockSpec(shape, lambda *_: (0,) * len(shape))


def struct(shape, dtype):
    return jax.ShapeDtypeStruct(shape, dtype)


def across(count, by):
    return [(i, (i // 8) * 8 + (i + 2 * by) % 8) for i in range(count)]


def shift_pairs(count, by):
    return [(i, i + by) for i in range(count) if 0 <= i + by < count]


def core_pairs(count):
    return [(i, i ^ 1) for i in range(count)]


def chip_index():
    return lax.rem(lax.axis_index("seq"), 8) // 2


def pack(arrays, widths):
    rows = arrays[0].shape[0]
    total = sum(widths)
    count = len(arrays)

    def kernel(*refs):
        ins, outs = refs[:count], refs[count:]
        for k in range(4):
            head = (chip_index() + k) & 3
            at = 0
            for ref, width in zip(ins, widths):
                first = pl.multiple_of(head * width, 128)
                outs[k][:, at : at + width] = ref[:, pl.ds(first, width)]
                at += width

    return pl.pallas_call(
        kernel,
        out_shape=[struct((rows, total), BF)] * 4,
        cost_estimate=pl.CostEstimate(
            flops=0, bytes_accessed=2 * rows * total * 8, transcendentals=0
        ),
        compiler_params=pltpu.CompilerParams(vmem_limit_bytes=12 * MB),
        name="pack",
    )(*arrays)


def positive(x):
    x = x.astype(F32)
    return jnp.where(x > 0, x + 1.0, jnp.exp(jnp.minimum(x, 0.0))).astype(BF)


def two_terms(x):
    high = x.astype(BF)
    return high, (x - high.astype(F32)).astype(BF)


def with_deltas(parts):
    def kernel(*refs):
        out, first_ref = refs[4:]
        sums = [jnp.zeros((HDIM, HDIM), F32) for _ in range(2)]
        norms = [jnp.zeros((1, HDIM), F32) for _ in range(2)]
        for k in range(4):
            block = refs[k][...]
            if k:
                out[(k - 1) * BLK : k * BLK, :] = block
            feat = positive(block[:, :HDIM])
            product = lax.dot_general(
                feat, block[:, HDIM:], (((0,), (0,)), ((), ())), preferred_element_type=F32
            )
            norm = jnp.sum(feat.astype(F32), axis=0, keepdims=True)
            half = ((chip_index() - k) & 3) // 2
            for n in range(2):
                sums[n] = sums[n] + jnp.where(half == n, product, 0.0)
                norms[n] = norms[n] + jnp.where(half == n, norm, 0.0)
        total = (sums[0] + sums[1]).astype(BF)
        at, half = 3 * BLK, HDIM // 2
        out[at : at + half, :HDIM] = total[:half]
        out[at : at + half, HDIM:] = total[half:]
        high, low = two_terms(jnp.broadcast_to(norms[0] + norms[1], (REST - at - half, HDIM)))
        out[at + half :, :HDIM] = high
        out[at + half :, HDIM:] = low
        first_ref[:HDIM, :] = sums[0]
        first_ref[HDIM:, :] = jnp.broadcast_to(norms[0], (MEM - HDIM, HDIM))

    return pl.pallas_call(
        kernel,
        out_shape=[struct((REST, 2 * HDIM), BF), struct((MEM, HDIM), F32)],
        cost_estimate=pl.CostEstimate(
            flops=2 * SEG * HDIM * HDIM, bytes_accessed=8 * SEG * HDIM * 2, transcendentals=0
        ),
        compiler_params=pltpu.CompilerParams(vmem_limit_bytes=12 * MB),
        name="with_deltas",
    )(*parts)


def near_sums(rests):
    half = HDIM // 2

    def kernel(*refs):
        three_ref, near_ref = refs[6:]

        def delta(age):
            memory = jnp.zeros((HDIM, HDIM), F32)
            norm = jnp.zeros((MEM - HDIM, HDIM), F32)
            for ref in (refs[age], refs[3 + age]):
                value = ref[:half, :].astype(F32)
                memory = memory + jnp.concatenate([value[:, :HDIM], value[:, HDIM:]], axis=0)
                value = ref[half : half + 8, :].astype(F32)
                norm = norm + (value[:, :HDIM] + value[:, HDIM:])
            return jnp.concatenate([memory, norm], axis=0)

        before = delta(1) + delta(2)
        near_ref[...] = before
        three_ref[...] = before + delta(0)

    spec = pl.BlockSpec((TAIL, 2 * HDIM), lambda i: (3 * BLK // TAIL, 0))
    return pl.pallas_call(
        kernel,
        grid=(1,),
        in_specs=[spec] * 6,
        out_specs=[whole((MEM, HDIM))] * 2,
        out_shape=[struct((MEM, HDIM), F32)] * 2,
        cost_estimate=pl.CostEstimate(flops=0, bytes_accessed=2 * MB, transcendentals=0),
        compiler_params=pltpu.CompilerParams(vmem_limit_bytes=12 * MB),
        name="near_sums",
    )(*rests)


def in_order(info, rows_mine, rows_other):
    def kernel(info_ref, *refs):
        mine_refs, other_refs, (k_all, v_all) = refs[:6], refs[6:12], refs[12:]
        chip, core, row = info_ref[0], info_ref[1], info_ref[2]
        lane = lax.broadcasted_iota(jnp.int32, (ROW, HDIM), 1)
        for age in range(BACK + 1):
            for k in range(4):
                block = slice(0, BLK) if k == 0 else slice((k - 1) * BLK, k * BLK)
                for part, c in ((mine_refs, core), (other_refs, 1 - core)):
                    ref = part[2 * age + (k > 0)]
                    place = 2 * ((chip - k) & 3) + c
                    at = pl.multiple_of((BACK - age) * ROW + place * BLK, BLK)
                    k_all[pl.ds(at, BLK), :HDIM] = ref[block, :HDIM]
                    v_all[pl.ds(at, BLK), :HDIM] = ref[block, HDIM:]
            bias = jnp.where(row >= age, 0.0, -1e30).astype(F32)
            at = pl.ds((BACK - age) * ROW, ROW)
            k_all[at, HDIM:] = jnp.where(lane == 0, bias, 0.0).astype(BF)
        v_all[:, HDIM:] = jnp.ones((SPAN, HDIM), BF)

    return pl.pallas_call(
        kernel,
        grid_spec=pltpu.PrefetchScalarGridSpec(
            num_scalar_prefetch=1,
            grid=(1,),
            in_specs=[whole(v.shape) for v in (*rows_mine, *rows_other)],
            out_specs=[whole((SPAN, 2 * HDIM))] * 2,
        ),
        out_shape=[struct((SPAN, 2 * HDIM), BF)] * 2,
        compiler_params=pltpu.CompilerParams(vmem_limit_bytes=24 * MB),
        cost_estimate=pl.CostEstimate(flops=0, bytes_accessed=9 * MB, transcendentals=0),
        name="in_order",
    )(info, *rows_mine, *rows_other)


def mixed_heads(info, gates, queries, both, memory, first, count, rounds, given=None):
    rows = GROUP * count
    number = len(rounds)
    lowest = rounds[0]

    def kernel(info_ref, gate_ref, *refs):
        q_refs, refs = refs[:number], refs[number:]
        k_all, v_all, refs = refs[0], refs[1], refs[2:]
        if memory:
            near_ref, far_refs, first_refs, refs = refs[0], refs[1:3], refs[3:5], refs[5:]
        if given is not None:
            given_ref, refs = refs[0], refs[1:]
        out_refs = refs[:number]
        q_now, o_now, local_now = refs[number:]
        step = pl.program_id(0)
        chip, core = info_ref[0], info_ref[1]
        source = (chip - step - lowest) & 3

        for k in range(number):

            @pl.when(step == k)
            def _(k=k):
                q_now[...] = q_refs[k][first : first + count, :]

        base = pl.multiple_of((2 * source + core) * BLK + first, 64)
        q_bare = jnp.concatenate(
            [q_now[:, g * HDIM : (g + 1) * HDIM] for g in range(GROUP)], axis=0
        )
        lane = lax.broadcasted_iota(jnp.int32, (rows, HDIM), 1)
        q = jnp.concatenate([q_bare, jnp.where(lane == 0, 1.0, 0.0).astype(BF)], axis=1)

        def keys_at(offset, size):
            return k_all[pl.ds(pl.multiple_of(base + offset, 64), size), :]

        def values_at(offset, size):
            return v_all[pl.ds(pl.multiple_of(base + offset, 64), size), :]

        def scores(offset, size):
            return lax.dot_general(q, keys_at(offset, size), LAST, preferred_element_type=F32)

        def summed(p, offset, size):
            return jnp.dot(p, values_at(offset, size), preferred_element_type=F32)

        def attended():
            token = lax.broadcasted_iota(jnp.int32, (rows, count), 0) & (count - 1)
            newer = lax.broadcasted_iota(jnp.int32, (rows, count), 1) <= token
            k_ends = jnp.concatenate([keys_at(0, count), keys_at(WINDOW, count)], axis=0)
            v_ends = jnp.concatenate([values_at(0, count), values_at(WINDOW, count)], axis=0)
            s = lax.dot_general(q, k_ends, LAST, preferred_element_type=F32)
            s = jnp.where(newer, s[:, count:], s[:, :count])
            top = jnp.max(s, axis=1, keepdims=True)
            p = jnp.exp2((s - top) * SCALE)
            p = jnp.concatenate([jnp.where(newer, 0.0, p), jnp.where(newer, p, 0.0)], axis=1)
            acc = jnp.dot(p.astype(BF), v_ends, preferred_element_type=F32)
            at = count
            while at < WINDOW:
                size = min(KEYS_STEP, WINDOW - at)
                s = scores(at, size)
                newest = jnp.maximum(top, jnp.max(s, axis=1, keepdims=True))
                p = jnp.exp2((s - newest) * SCALE).astype(BF)
                acc = acc * jnp.exp2((top - newest) * SCALE) + summed(p, at, size)
                top = newest
                at += size
            return acc[:, :HDIM] / acc[:, HDIM:]

        if not memory:
            out_refs[0][...] = attended()
            return
        if given is None:
            local = attended()
        else:

            @pl.when(step == 0)
            def _():
                local_now[...] = given_ref[...]

            @pl.when(step != 0)
            def _():
                local_now[...] = attended()

            local = local_now[...]

        feat = positive(q_bare)
        half = source // 2
        known = near_ref[...] + far_refs[0][...] + far_refs[1][...]
        first_half = first_refs[0][...] + first_refs[1][...]
        known = known + jnp.where(half == 1, first_half, 0.0)
        mem_high, mem_low = two_terms(known[:HDIM])
        recalled = jnp.dot(feat, mem_high, preferred_element_type=F32)
        recalled = recalled + jnp.dot(feat, mem_low, preferred_element_type=F32)
        norm = jnp.broadcast_to(known[HDIM : HDIM + 1], (HDIM, HDIM))
        norm_high, norm_low = two_terms(norm)
        below = lax.dot_general(feat, norm_high, LAST, preferred_element_type=F32)
        below = below + lax.dot_general(feat, norm_low, LAST, preferred_element_type=F32)
        retrieved = recalled / (1.0 + below)
        for g in range(GROUP):
            share = jax.nn.sigmoid(jnp.full((1, HDIM), gate_ref[chip * GROUP + g], F32))
            at = slice(g * count, (g + 1) * count)
            value = share * retrieved[at] + (1.0 - share) * local[at]
            o_now[:, g * HDIM : (g + 1) * HDIM] = value.astype(BF)
        for k in range(number):

            @pl.when(step == k)
            def _(k=k):
                out_refs[k][...] = o_now[...]

    extra = [*memory] + ([given] if given is not None else [])
    out = struct((count, GROUP * HDIM), BF) if memory else struct((rows, HDIM), F32)
    return pl.pallas_call(
        kernel,
        grid_spec=pltpu.PrefetchScalarGridSpec(
            num_scalar_prefetch=1,
            grid=(number,),
            in_specs=[pl.BlockSpec(memory_space=pltpu.SMEM)]
            + [whole((BLK, GROUP * HDIM))] * number
            + [whole((SPAN, 2 * HDIM))] * 2
            + [whole(a.shape) for a in extra],
            out_specs=[whole(out.shape)] * number,
            scratch_shapes=[
                pltpu.VMEM((count, GROUP * HDIM), BF),
                pltpu.VMEM((count, GROUP * HDIM), BF),
                pltpu.VMEM((rows, HDIM), F32),
            ],
        ),
        out_shape=[out] * number,
        compiler_params=pltpu.CompilerParams(vmem_limit_bytes=28 * MB),
        cost_estimate=pl.CostEstimate(
            flops=4 * number * rows * WINDOW * HDIM * 4,
            bytes_accessed=4 * MB,
            transcendentals=number * rows * WINDOW,
        ),
        name="mixed_heads",
    )(info, gates, *[queries[k] for k in rounds], *both, *extra)


def projected(info, mixed, weight, side, dtype):
    count = mixed[0].shape[0]
    depth, width = weight.shape
    tile = 512
    tiles = width // 2 // tile

    def kernel(info_ref, a, b, c, d, w_ref, out_ref, held):
        @pl.when(pl.program_id(0) == 0)
        def _():
            for k, ref in enumerate((a, b, c, d)):
                head = (info_ref[0] + k) & 3
                at = pl.multiple_of(head * GROUP * HDIM, 128)
                held[:, pl.ds(at, GROUP * HDIM)] = ref[...]

        out_ref[...] = jnp.dot(held[...], w_ref[...], preferred_element_type=F32).astype(dtype)

    return pl.pallas_call(
        kernel,
        grid_spec=pltpu.PrefetchScalarGridSpec(
            num_scalar_prefetch=1,
            grid=(tiles,),
            in_specs=[whole((count, GROUP * HDIM))] * 4
            + [pl.BlockSpec((depth, tile), lambda n, info: (0, (info[3] ^ side) * tiles + n))],
            out_specs=pl.BlockSpec((count, tile), lambda n, info: (0, n)),
            scratch_shapes=[pltpu.VMEM((count, depth), BF)],
        ),
        out_shape=struct((count, width // 2), dtype),
        compiler_params=pltpu.CompilerParams(vmem_limit_bytes=24 * MB),
        cost_estimate=pl.CostEstimate(
            flops=2 * count * depth * width // 2, bytes_accessed=depth * width, transcendentals=0
        ),
        name="projected",
    )(info, *mixed, weight)


def per_device(queries, keys, values, gate_logit, out_weight):
    size = lax.axis_size("seq")
    seq = lax.axis_index("seq")
    side = lax.axis_index("head")
    row, core = seq // 8, seq % 2
    info = jnp.stack([(seq % 8) // 2, core, row, side]).astype(jnp.int32)
    gates = gate_logit.astype(F32)

    def moved(value, pairs):
        return lax.ppermute(value, "seq", pairs)

    def to_chips(parts, sign):
        return [parts[0]] + [moved(parts[k], across(size, sign * k)) for k in (1, 2, 3)]

    kv_out = pack((keys, values), (HDIM, HDIM))
    kv_in = to_chips(kv_out, 1)
    q_out = pack((queries,), (GROUP * HDIM,))
    if EARLY:
        early = [moved(kv_out[0], shift_pairs(size, 8 * by)) for by in (1, 2)]
        tied = lax.optimization_barrier((*kv_in, *early, *q_out))
        kv_in, early, q_out = tied[:4], tied[4:6], tied[6:]
    else:
        tied = lax.optimization_barrier((*kv_in, *q_out))
        kv_in, q_out = tied[:4], tied[4:]
        early = [moved(kv_in[0], shift_pairs(size, 8 * by)) for by in (1, 2)]
    rest, first = with_deltas(kv_in)
    own = (kv_in[0], rest)
    last = (early[0], moved(own[1], shift_pairs(size, 8)))
    older = (early[1], moved(own[1], shift_pairs(size, 16)))
    q_in = to_chips(q_out, 1)
    tied = lax.optimization_barrier((*last, *older, *q_in[1:]))
    last, older, q_in[1:] = tied[:2], tied[2:4], tied[4:]

    mine = (*own, *last, *older)
    other = tuple(moved(v, core_pairs(size)) for v in mine)
    three, near = near_sums((*mine[1::2], *other[1::2]))
    firsts = (first, moved(first, core_pairs(size)))
    both = in_order(info, mine, other)
    far = [moved(three, shift_pairs(size, by)) for by in (24, 48)]
    memory = (near, *far, *firsts)

    def heads(which, chunk, rounds, memory, given=None):
        first, count = CHUNKS[chunk]
        return mixed_heads(
            info, gates, which, both, memory, first, count, rounds, given
        )

    def back(part, k):
        return moved(part, across(size, -k)) if k else part

    def swapped(value):
        return lax.ppermute(value, "head", [(0, 1), (1, 0)])

    zero, one, two, three = heads(q_in, 0, (0, 1, 2, 3), memory)
    parts = [zero, back(one, 1), back(two, 2), back(three, 3)]
    ahead = heads(q_in, 1, (1, 2, 3), memory)
    tied = lax.optimization_barrier((*parts, *ahead))
    parts, ahead = tied[:4], tied[4:]
    theirs = projected(info, parts, out_weight, 1, BF)
    theirs, q_self = lax.optimization_barrier((theirs, q_in[0]))
    later = [back(ahead[k - 1], k) for k in (1, 2, 3)]
    arrived = swapped(theirs)
    later = [*heads([q_self], 1, (0,), memory), *later]
    theirs_later = projected(info, later, out_weight, 1, BF)
    arrived_later = swapped(theirs_later)
    tied = lax.optimization_barrier((*parts, theirs_later))
    first = projected(info, tied[:4], out_weight, 0, F32) + arrived.astype(F32)
    second = projected(info, later, out_weight, 0, F32) + arrived_later.astype(F32)
    return jnp.concatenate([first.astype(BF), second.astype(BF)], axis=0)


def solution(mesh):
    in_specs = (P("seq", "head"), P("seq", "head"), P("seq", "head"), P("head"), P("head", None))
    return jax.shard_map(
        per_device, mesh=mesh, in_specs=in_specs, out_specs=P("seq", "head"), check_vma=False
    )
```
